32 devices in a mesh: groups: 2 (over y), expert: 8 (over z, x), dp: 2 (over core).
Axes of the slice: x: 2, y: 2, z: 4, core: 2. Of those that a mesh axis runs over, the one named last changes fastest.
Arguments:
- queries: bfloat16 [128, 8, 576], P(('groups', 'dp'), 'expert'), parts along dimension 0, may hold values from -400 to 400
- kv_pages: bfloat16 [128, 64, 576], P(('groups', 'dp')), parts along dimension 0, may hold values from -10 to 10
- page_tables: int32 [128, 8], P(('groups', 'dp')), parts along dimension 0, may hold values from 0 to 31, as said below
- lengths: int32 [128], P(('groups', 'dp')), parts along dimension 0, may hold values from 2 to 512
- owners: int32 [128], P(('groups', 'dp')), parts along dimension 0, may hold values from 0 to 7, as said below
- up_values: bfloat16 [8, 512, 128], P('expert'), may hold values from -0.25 to 0.25
- out_proj: bfloat16 [8, 128, 3584], P('expert'), may hold values from -0.1875 to 0.1875
- residual: bfloat16 [128, 3584], P(('groups', 'expert', 'dp')), parts along dimension 0, may hold values from -0.59765625 to 0.59765625
- verify_states: bfloat16 [128, 2, 3584], P(('groups', 'expert', 'dp')), parts along dimension 0, may hold values from -6 to 6
- norm_gain: bfloat16 [3584], replicated, may hold values from 0.099609375 to 1.8984375
- route_ids: int32 [128, 3, 8], P(('groups', 'expert', 'dp')), parts along dimension 0, may hold values from 0 to 15, all different within a row; in each aligned block of 12 rows (0 to 11, 12 to 23, ..., all dimensions but the last counted through in order) at most 12 rows name the same one
- route_weights: float32 [128, 3, 8], P(('groups', 'expert', 'dp')), parts along dimension 0, may hold values from 0.05 to 1
- expert_up: bfloat16 [16, 3584, 1024], P(('expert', 'dp')), may hold values from -0.09375 to 0.09375
Outputs:
- moe_slots: bfloat16 [128, 3, 8, 1024], P(('groups', 'expert', 'dp')), parts along dimension 0
The draws below stay inside these ranges and needn't reach their ends.
There are 2 independent parts, one for each index of `groups`. The reference program is written for one: setup_inputs(seed, part) draws one part's arguments, and reference() takes and returns one part's arrays. A program takes and returns all parts, laid end to end along the dimension named above; an argument that names none is the same for every part. Nothing has to cross between parts.
Inputs may be any that keep to these rules, and one draw needn't show every extreme that they name: `page_tables`: each row names 8 different pages, numbered within its block of 32 rows. `owners`: in each block of 32 rows every owner is named exactly 4 times. `route_ids`: A token's 8 experts differ; in the rows of one device no expert is named more than 12 times.
All inputs are finite; a program needn't handle non-finite values.
Results may differ from the reference program's by a relative error of at most 0.0064.
Values may be sent and summed in bfloat16 or wider, within the bound.
No kernel may reach another device: no remote copies, remote signals or barrier semaphores. Data moves between devices by JAX's collectives and lax.ppermute only.
A program may use at most 64 MiB of HBM per device.

```python
import math
import jax
import jax.numpy as jnp
import numpy as np
from jax import lax

D = 3584
LATENT = 512
ROPE = 64
VHEAD = 128
KDIM = 576
HEADS = 8
HE = 1024
TOPK = 8
VERIFY = 3
PAGE = 64
TABLE = 8
PAGES_DP = 32
ROWS_DEV = 4
ROWS_DP = 32
ROWS = 64
PAGES = 64
EXPERTS = 16
CAP = 12
N_EXPERT = 8
N_DP = 2


def table_draw(key):
    row_keys = jax.random.split(jax.random.fold_in(key, 101), ROWS)
    return jax.vmap(lambda row_key: jax.random.permutation(row_key, PAGES_DP)[:TABLE])(row_keys).astype(jnp.int32)


def rotary_draw(key):
    return jax.random.normal(jax.random.fold_in(key, 102), (PAGES, PAGE, ROPE), jnp.float32)


def draw_page_tables(key, part):
    return table_draw(key)


def draw_kv_pages(key, part):
    rotary = rotary_draw(key)
    key = jax.random.fold_in(key, 2)
    latent = jax.random.normal(key, (PAGES, PAGE, LATENT), jnp.float32)
    return jnp.concatenate([latent, rotary], axis=-1).astype(jnp.bfloat16)


def draw_queries(key, part):
    key = jax.random.fold_in(key, 4)
    base = jax.random.normal(key, (ROWS, HEADS, KDIM), jnp.float32)
    return base.astype(jnp.bfloat16)


def draw_lengths(key, part):
    key = jax.random.fold_in(key, 6)
    drawn = jax.random.randint(key, (ROWS,), 2, TABLE * PAGE + 1, jnp.int32)
    return drawn.at[0].set(TABLE * PAGE)


def draw_owners(key, part):
    key = jax.random.fold_in(key, 7)
    half_keys = jax.random.split(key, N_DP)
    shuffled = jax.vmap(lambda half_key: jax.random.permutation(half_key, ROWS_DP))(half_keys)
    return (shuffled // ROWS_DEV).reshape(ROWS).astype(jnp.int32)


def steps_of(own_key, extent, pieces, low, largest):
    loudness, own = 1.0, jax.random.fold_in(own_key, 6)
    for dim, blocks in pieces:
        steps = jnp.exp(jax.random.uniform(jax.random.fold_in(own, dim), (blocks,), jnp.float32, low / len(pieces), largest / len(pieces)))
        loudness = loudness * jnp.repeat(steps, extent[dim] // blocks).reshape([-1 if axis == dim else 1 for axis in range(len(extent))])
    return loudness


def deal_out(rng, own, number, rows, count, top, limit, skew):
    sequence = jax.random.permutation(rng, count)
    crowded, common = portions_of(count, rows * top, limit, skew, True), portions_of(count, rows * top, limit, skew, False)
    places = jnp.arange(count)

    def named(tallies, offset_by):
        used = int((tallies > 0).sum())
        fixed = max(1, used // 4)
        moved = fixed + (places - fixed + offset_by * (used - fixed)) % max(1, count - fixed)
        return jnp.zeros((count,), jnp.int32).at[sequence[jnp.where(places < fixed, places, moved)]].set(jnp.asarray(tallies, jnp.int32))

    tallies = jnp.where(number % 4 == 0, named(crowded, number // 4), named(common, number - number // 4 - 1))
    mixed = jax.random.permutation(jax.random.fold_in(own, 3), count)
    giver, receiver = mixed[0:count // 2 * 2:2], mixed[1:count // 2 * 2:2]
    slack = jnp.minimum(tallies[giver] - 1, limit - tallies[receiver]) // 2
    slack = jnp.where((giver == sequence[0]) | (receiver == sequence[0]) | (tallies[receiver] == 0), 0, jnp.maximum(slack, 0))
    moved = jax.random.randint(jax.random.fold_in(own, 4), (count // 2,), 0, 1 << 20) % (slack + 1)
    tallies = tallies.at[giver].add(-moved).at[receiver].add(moved)
    members = jnp.searchsorted(jnp.cumsum(tallies), jnp.arange(rows * top), side="right").astype(jnp.int32)
    table = members.reshape(top, rows).T
    table = table[jax.random.permutation(jax.random.fold_in(own, 1), rows)]
    offset_by = jax.random.randint(jax.random.fold_in(own, 2), (rows, 1), 0, top)
    return jnp.take_along_axis(table, (jnp.arange(top)[None, :] + offset_by) % top, axis=1)


def portions_of(number_of, total, bound, slope, full):
    weights = [(1 << 20) // math.isqrt(standing ** slope) + 1 for standing in range(1, number_of + 1)]
    largest = bound if full else min(bound, max(-(-total // number_of), total * weights[0] // sum(weights)))
    least = 1 if total - largest >= number_of - 1 else 0
    holding, spare = [largest] + [least] * (number_of - 1), total - largest - least * (number_of - 1)
    while spare > 0:
        movable = [i for i in range(1, number_of) if holding[i] < largest] or [i for i in range(1, number_of) if holding[i] < bound]
        whole, budget = sum([weights[i] for i in movable]), spare
        for i in movable:
            extra = min(bound - holding[i], max(1, budget * weights[i] // whole), spare)
            holding[i] = holding[i] + extra
            spare = spare - extra
    return np.array(holding)


def normal_values(own_key, shape, spread, most, pieces=(), kind=jnp.bfloat16):
    values = spread * jax.random.normal(own_key, shape, jnp.float32)
    if pieces:
        values = values * steps_of(own_key, shape, pieces, -0.22, 0.18)
    return jnp.clip(values, -most, most).astype(kind)


def setup_inputs(seed: int = 0, part: int = 0) -> dict:
    splits = jax.random.split(jax.random.key(seed), 14)
    own_keys = jax.random.split(jax.random.fold_in(splits[13], part), 14)
    queries = draw_queries(jax.random.fold_in(jax.random.fold_in(splits[13], part), 71), part)
    kv_pages = draw_kv_pages(jax.random.fold_in(jax.random.fold_in(splits[13], part), 71), part)
    page_tables = draw_page_tables(jax.random.fold_in(jax.random.fold_in(splits[13], part), 71), part)
    lengths = draw_lengths(jax.random.fold_in(jax.random.fold_in(splits[13], part), 71), part)
    owners = draw_owners(jax.random.fold_in(jax.random.fold_in(splits[13], part), 71), part)
    up_values = normal_values(splits[5], (HEADS, LATENT, VHEAD), LATENT ** -0.5, 0.25, ((0, 8),))
    out_proj = normal_values(splits[6], (HEADS, VHEAD, D), (HEADS * VHEAD) ** -0.5, 0.1875, ((0, 8),))
    residual = normal_values(own_keys[7], (ROWS, D), 0.1, 0.59765625, ((0, 16),))
    verify_states = normal_values(own_keys[8], (ROWS, VERIFY - 1, D), 1.0, 6.0, ((0, 16),))
    norm_gain = jnp.clip(1.0 + 0.18 * jax.random.normal(splits[9], (D,), jnp.float32), 0.099609375, 1.8984375).astype(jnp.bfloat16)
    route_ids_keys = jax.random.split(jax.random.fold_in(own_keys[10], 1), ROWS * VERIFY // (VERIFY * ROWS_DEV))
    route_ids_turns = jax.random.permutation(jax.random.fold_in(own_keys[10], 3), ROWS * VERIFY // (VERIFY * ROWS_DEV))
    route_ids = jax.vmap(lambda own, number: deal_out(jax.random.fold_in(own_keys[10], 2), own, number, VERIFY * ROWS_DEV, EXPERTS, TOPK, CAP, 2))(route_ids_keys, route_ids_turns).reshape((ROWS, VERIFY, TOPK))
    route_weights = jnp.clip(jnp.exp(math.log(1.0) - 2.9957323 * jax.random.uniform(own_keys[11], (ROWS, VERIFY, TOPK), jnp.float32) ** steps_of(own_keys[11], (ROWS, VERIFY, TOPK), ((0, 16),), -0.2, 0.2)), 0.05, 1.0)
    expert_up = normal_values(splits[12], (EXPERTS, D, HE), D ** -0.5, 0.09375, ((0, 16),))
    return dict(queries=queries, kv_pages=kv_pages, page_tables=page_tables, lengths=lengths, owners=owners, up_values=up_values, out_proj=out_proj, residual=residual, verify_states=verify_states, norm_gain=norm_gain, route_ids=route_ids, route_weights=route_weights, expert_up=expert_up)


def block_values(query_block, table_block, length_block, pages, up_head):
    page_total, page_len, key_width = pages.shape
    table_len = table_block.shape[1]
    present = table_block[:, :, None] == jnp.arange(page_total, dtype=jnp.int32)[None, None, :]
    slot_index = lax.optimization_barrier(jnp.sum(jnp.where(present, jnp.arange(table_len, dtype=jnp.int32)[None, :, None], 0), axis=1))
    member = jnp.any(present, axis=1)
    positions = slot_index[:, :, None] * page_len + jnp.arange(page_len, dtype=jnp.int32)[None, None, :]
    visible = member[:, :, None] & (positions < length_block[:, None, None])
    visible = visible.reshape(query_block.shape[0], page_total * page_len)
    keys_flat = pages.reshape(page_total * page_len, key_width)
    scores = jnp.dot(query_block, keys_flat.T, preferred_element_type=jnp.float32) * (VHEAD + ROPE) ** (-0.5)
    masked = jnp.where(visible, scores, -1e+30)
    row_max = lax.optimization_barrier(jnp.max(masked, axis=1, keepdims=True))
    exponent = jnp.where(visible, jnp.exp(masked - row_max), 0.0)
    attention = (exponent / lax.optimization_barrier(jnp.sum(exponent, axis=1, keepdims=True))).astype(jnp.bfloat16)
    context = jnp.dot(attention, keys_flat[:, :LATENT], preferred_element_type=jnp.float32).astype(jnp.bfloat16)
    return jnp.dot(context, up_head, preferred_element_type=jnp.float32).astype(jnp.bfloat16)

def reference(queries, kv_pages, page_tables, lengths, owners, up_values, out_proj, residual, verify_states, norm_gain, route_ids, route_weights, expert_up):
    blocks = []
    for half_index in range(N_DP):
        first_row = half_index * ROWS_DP
        pages_half = kv_pages[half_index * PAGES_DP:(half_index + 1) * PAGES_DP]
        queries_half = queries[first_row:first_row + ROWS_DP]
        tables_half = page_tables[first_row:first_row + ROWS_DP]
        lengths_half = lengths[first_row:first_row + ROWS_DP]

        def one_head(inputs):
            query_head, up_head = inputs
            return block_values(query_head, tables_half, lengths_half, pages_half, up_head)
        per_head = lax.map(one_head, (jnp.swapaxes(queries_half, 0, 1), up_values))
        flattened = jnp.swapaxes(per_head, 0, 1).reshape(ROWS_DP, HEADS * VHEAD)
        summed = jnp.dot(flattened, out_proj.reshape(HEADS * VHEAD, D), preferred_element_type=jnp.float32)
        row_order = jnp.argsort(owners[first_row:first_row + ROWS_DP], stable=True)
        blocks.append(summed[row_order].reshape(N_EXPERT, ROWS_DEV, D))
    gathered_hidden = jnp.stack(blocks, axis=1).reshape(ROWS, D)
    states = jnp.concatenate([(residual.astype(jnp.float32) + gathered_hidden)[:, None, :], verify_states.astype(jnp.float32)], axis=1)
    normed = states * lax.rsqrt(lax.optimization_barrier(jnp.mean(states * states, axis=-1, keepdims=True)) + 1e-06) * norm_gain.astype(jnp.float32)
    token_rows = normed.astype(jnp.bfloat16).reshape(ROWS * VERIFY, D)
    slot_total = ROWS * VERIFY * TOPK
    route_flat = route_ids.reshape(slot_total)
    padded = jnp.concatenate([token_rows, jnp.zeros((1, D), jnp.bfloat16)], axis=0)
    most_rows = EXPERTS * CAP

    def one_expert(expert_index):
        chosen = route_flat == expert_index
        slot_list = jnp.nonzero(chosen, size=most_rows, fill_value=slot_total)[0].astype(jnp.int32)
        rows_in = padded[slot_list // TOPK]
        weight_here = lax.dynamic_index_in_dim(expert_up, expert_index, 0, keepdims=False)
        product = jnp.dot(rows_in, weight_here, preferred_element_type=jnp.float32)
        return (slot_list, jax.nn.silu(product).astype(jnp.bfloat16))
    slot_lists, activations = lax.map(one_expert, jnp.arange(EXPERTS, dtype=jnp.int32))
    gathered = jnp.zeros((slot_total + 1, HE), jnp.bfloat16).at[slot_lists.reshape(-1)].set(activations.reshape(-1, HE))[:slot_total]
    weighted = route_weights.reshape(slot_total, 1) * gathered.astype(jnp.float32)
    return weighted.astype(jnp.bfloat16).reshape(ROWS, VERIFY, TOPK, HE)
```

```python
import functools

import jax
import jax.numpy as jnp
from jax import lax
from jax.experimental import pallas as pl
from jax.experimental.pallas import tpu as pltpu
from jax.sharding import PartitionSpec as P

LATENT = 512
ROPE = 64
VHEAD = 128
VERIFY = 3
BF = jnp.bfloat16
F32 = jnp.float32
VMEM = pl.BlockSpec(memory_space=pltpu.VMEM)


def params(mib=40):
    return pltpu.CompilerParams(vmem_limit_bytes=mib * 1024 * 1024)


def as_column(row, size):
    eye = lax.broadcasted_iota(jnp.int32, (size, size), 0) == lax.broadcasted_iota(
        jnp.int32, (size, size), 1
    )
    return jnp.sum(jnp.where(eye, row, 0), axis=1, keepdims=True)


def attention_kernel(per_owner, q_ref, kv_ref, table_ref, length_ref, owner_ref, up_ref, out_ref, sum_ref):
    rows = q_ref.shape[0]
    tokens = kv_ref.shape[0]
    slots = table_ref.shape[0]
    page_len = 64
    token = lax.broadcasted_iota(jnp.int32, (1, tokens), 1)
    page, offset = token // page_len, token % page_len
    position = jnp.full((rows, tokens), 1 << 24, jnp.int32)
    for slot in range(slots):
        named = as_column(table_ref[slot : slot + 1, :], rows)
        position = jnp.where(named == page, slot * page_len + offset, position)
    visible = position < as_column(length_ref[...], rows)
    scores = lax.dot_general(
        q_ref[...], kv_ref[...], (((1,), (1,)), ((), ())), preferred_element_type=F32
    ) * (VHEAD + ROPE) ** (-0.5)
    masked = jnp.where(visible, scores, -1e30)
    row_max = jnp.max(masked, axis=1, keepdims=True)
    exponent = jnp.where(visible, jnp.exp(masked - row_max), 0.0)
    attention = (exponent / jnp.sum(exponent, axis=1, keepdims=True)).astype(BF)
    context = jnp.dot(attention, kv_ref[:, :LATENT], preferred_element_type=F32).astype(BF)
    values = jnp.dot(context, up_ref[...], preferred_element_type=F32).astype(BF)
    owner = owner_ref[...]
    first = lax.broadcasted_iota(jnp.int32, (rows, rows), 0)
    second = lax.broadcasted_iota(jnp.int32, (rows, rows), 1)
    before = (as_column(owner, rows) == owner) & (first < second)
    target = owner * per_owner + jnp.sum(before.astype(jnp.int32), axis=0, keepdims=True)
    picked = jnp.dot((first == target).astype(BF), values, preferred_element_type=F32).astype(BF)
    summed = jnp.dot(picked, out_ref[...], preferred_element_type=F32).astype(BF)
    for e in range(rows // per_owner):
        sum_ref[e] = summed[e * per_owner : (e + 1) * per_owner]


def normed(states, gain):
    scale = lax.rsqrt(jnp.mean(states * states, axis=-1, keepdims=True) + 1e-06)
    return (states * scale * gain).astype(BF)


def norm_verify_kernel(states_ref, gain_ref, out_ref):
    gain = gain_ref[...].astype(F32)
    count = states_ref.shape[1]
    rows = [
        normed(states_ref[q].astype(F32), gain) for q in range(states_ref.shape[0])
    ]
    out_ref[...] = jnp.concatenate(rows, axis=0)


def norm_draft_kernel(copies, parts_ref, residual_ref, gain_ref, out_ref):
    states = residual_ref[...].astype(F32)
    total = parts_ref[0].astype(F32)
    for e in range(1, parts_ref.shape[0]):
        total = total + parts_ref[e].astype(F32)
    tokens = normed(states + total, gain_ref[...].astype(F32))
    for c in range(copies):
        out_ref[c] = tokens


def expert_kernel(codes, verify_ref, draft_ref, weight_ref, out_ref):
    me = lax.axis_index("expert") * lax.axis_size("dp") + lax.axis_index("dp")
    devices, per_draft, width = draft_ref.shape
    weight = weight_ref[...]
    product = jnp.dot(verify_ref[...], weight, preferred_element_type=F32)
    active = (product * jax.nn.sigmoid(product)).astype(BF)
    per_verify = active.shape[0] // devices
    for block, code in enumerate(codes):
        out_ref[me ^ code, per_draft:] = active[block * per_verify : (block + 1) * per_verify]
    draft = draft_ref[...].reshape(devices * per_draft, width)
    product = jnp.dot(draft, weight, preferred_element_type=F32)
    active = (product * jax.nn.sigmoid(product)).astype(BF)
    for d in range(devices):
        out_ref[d, :per_draft] = active[d * per_draft : (d + 1) * per_draft]


def select_kernel(order, ids_ref, gates_ref, back_ref, out_ref):
    devices, per, width = back_ref.shape
    top = ids_ref.shape[2]
    eye = lax.broadcasted_iota(jnp.int32, (top, top), 0) == lax.broadcasted_iota(
        jnp.int32, (top, top), 1
    )
    source = lax.broadcasted_iota(jnp.int32, (top, devices), 1)
    for t in range(ids_ref.shape[0]):
        for q in range(ids_ref.shape[1]):
            ids = jnp.sum(jnp.where(eye, ids_ref[t, q : q + 1, :], 0), axis=1, keepdims=True)
            gates = jnp.sum(
                jnp.where(eye, gates_ref[t, q : q + 1, :], 0.0), axis=1, keepdims=True
            )
            chosen = (ids == source).astype(BF)
            rows = back_ref[:, order(q, t), :]
            active = jnp.dot(chosen, rows, preferred_element_type=F32)
            out_ref[q, t] = (gates * active).astype(BF)


def swap(x, axis, size, mask):
    return lax.ppermute(x, axis, [(i, i ^ mask) for i in range(size)])


def per_device(queries, kv_pages, page_tables, lengths, owners, up_values, out_proj, residual,
               verify_states, norm_gain, route_ids, route_weights, expert_up):
    rows, _, key_width = queries.shape
    verify_rows, width = residual.shape
    n_expert, n_dp = lax.axis_size("expert"), lax.axis_size("dp")
    experts = n_expert * n_dp
    hidden = expert_up.shape[2]
    gain = norm_gain.reshape(1, width)

    verify_tokens = pl.pallas_call(
        norm_verify_kernel,
        out_shape=jax.ShapeDtypeStruct((verify_rows * (VERIFY - 1), width), BF),
        in_specs=[VMEM, VMEM],
        out_specs=VMEM,
        name="norm_verify",
        compiler_params=params(),
    )(verify_states, gain)

    partial_sums = pl.pallas_call(
        functools.partial(attention_kernel, verify_rows),
        out_shape=jax.ShapeDtypeStruct((n_expert, verify_rows, width), BF),
        in_specs=[VMEM] * 7,
        out_specs=VMEM,
        name="attention",
        compiler_params=params(),
    )(
        queries.reshape(rows, key_width),
        kv_pages.reshape(-1, key_width),
        page_tables.T,
        lengths.reshape(1, rows),
        owners.reshape(1, rows),
        up_values[0],
        out_proj[0],
    )

    gathered = verify_tokens
    codes = [0]
    mask = n_expert // 2
    while mask:
        gathered = jnp.concatenate([gathered, swap(gathered, "expert", n_expert, mask)], axis=0)
        codes += [code ^ (mask * n_dp) for code in codes]
        mask //= 2
    gathered = jnp.concatenate([gathered, swap(gathered, "dp", n_dp, 1)], axis=0)
    codes += [code ^ 1 for code in codes]

    parts = lax.all_to_all(partial_sums, "expert", split_axis=0, concat_axis=0, tiled=True)
    draft_tokens = pl.pallas_call(
        functools.partial(norm_draft_kernel, experts),
        out_shape=jax.ShapeDtypeStruct((experts, verify_rows, width), BF),
        in_specs=[VMEM] * 3,
        out_specs=VMEM,
        name="norm_draft",
        compiler_params=params(),
    )(parts, residual, gain)
    draft = lax.all_to_all(draft_tokens, ("expert", "dp"), split_axis=0, concat_axis=0, tiled=True)
    active = pl.pallas_call(
        functools.partial(expert_kernel, codes),
        out_shape=jax.ShapeDtypeStruct((experts, verify_rows * VERIFY, hidden), BF),
        in_specs=[VMEM] * 3,
        out_specs=VMEM,
        name="expert",
        compiler_params=params(),
    )(gathered, draft, expert_up[0])
    back = lax.all_to_all(active, ("expert", "dp"), split_axis=0, concat_axis=0, tiled=True)
    top = route_ids.shape[2]

    def order(q, t):
        return q if t == 0 else verify_rows + q * (VERIFY - 1) + t - 1

    return pl.pallas_call(
        functools.partial(select_kernel, order),
        out_shape=jax.ShapeDtypeStruct((verify_rows, VERIFY, top, hidden), BF),
        in_specs=[VMEM] * 3,
        out_specs=VMEM,
        name="select",
        compiler_params=params(),
    )(route_ids.transpose(1, 0, 2), route_weights.transpose(1, 0, 2), back)


def solution(mesh):
    placed = (
        P(("groups", "dp"), "expert", None),
        P(("groups", "dp"), None, None),
        P(("groups", "dp"), None),
        P(("groups", "dp")),
        P(("groups", "dp")),
        P("expert", None, None),
        P("expert", None, None),
        P(("groups", "expert", "dp"), None),
        P(("groups", "expert", "dp"), None, None),
        P(),
        P(("groups", "expert", "dp"), None, None),
        P(("groups", "expert", "dp"), None, None),
        P(("expert", "dp"), None, None),
    )
    return jax.shard_map(
        per_device,
        mesh=mesh,
        in_specs=placed,
        out_specs=P(("groups", "expert", "dp"), None, None, None),
        check_vma=False,
    )
```

```python
import functools

import jax
import jax.numpy as jnp
from jax import lax
from jax.experimental import pallas as pl
from jax.experimental.pallas import tpu as pltpu
from jax.sharding import PartitionSpec as P

LATENT = 512
ROPE = 64
VHEAD = 128
VERIFY = 3
PAGES = 32
NEAR = 2
CHUNKS = 7
ROW_BLOCK = 256
BF = jnp.bfloat16
F32 = jnp.float32
VMEM = pl.BlockSpec(memory_space=pltpu.VMEM)
HBM = pl.BlockSpec(memory_space=pltpu.HBM)


def params(mib=40):
    return pltpu.CompilerParams(vmem_limit_bytes=mib * 1024 * 1024)


def as_column(row, size):
    eye = lax.broadcasted_iota(jnp.int32, (size, size), 0) == lax.broadcasted_iota(
        jnp.int32, (size, size), 1
    )
    return jnp.sum(jnp.where(eye, row, 0), axis=1, keepdims=True)


def fetch(sources, targets, semaphores):
    copies = [
        pltpu.make_async_copy(source, target, semaphores.at[i])
        for i, (source, target) in enumerate(zip(sources, targets))
    ]
    for copy in copies:
        copy.start()
    return copies


def attention_kernel(per_owner, *refs):
    sources, sum_ref, targets, semaphores = refs[:7], refs[7], refs[8:15], refs[15]
    copies = fetch(sources, targets, semaphores)
    q_ref, kv_ref, table_ref, length_ref, owner_ref, up_ref, out_ref = targets
    rows = q_ref.shape[0]
    tokens = kv_ref.shape[0]
    slots = table_ref.shape[0]
    page_len = tokens // PAGES
    token = lax.broadcasted_iota(jnp.int32, (1, tokens), 1)
    page, offset = token // page_len, token % page_len
    position = jnp.full((rows, tokens), 1 << 24, jnp.int32)
    for copy in copies[2:5]:
        copy.wait()
    for slot in range(slots):
        named = as_column(table_ref[slot : slot + 1, :], rows)
        position = jnp.where(named == page, slot * page_len + offset, position)
    visible = position < as_column(length_ref[...], rows)
    owner = owner_ref[...]
    first = lax.broadcasted_iota(jnp.int32, (rows, rows), 0)
    second = lax.broadcasted_iota(jnp.int32, (rows, rows), 1)
    before = (as_column(owner, rows) == owner) & (first < second)
    target = owner * per_owner + jnp.sum(before.astype(jnp.int32), axis=0, keepdims=True)
    for copy in copies[:2]:
        copy.wait()
    scores = lax.dot_general(
        q_ref[...], kv_ref[...], (((1,), (1,)), ((), ())), preferred_element_type=F32
    ) * (VHEAD + ROPE) ** (-0.5)
    masked = jnp.where(visible, scores, -1e30)
    row_max = jnp.max(masked, axis=1, keepdims=True)
    exponent = jnp.where(visible, jnp.exp(masked - row_max), 0.0)
    attention = (exponent / jnp.sum(exponent, axis=1, keepdims=True)).astype(BF)
    context = jnp.dot(attention, kv_ref[:, :LATENT], preferred_element_type=F32).astype(BF)
    for copy in copies[5:]:
        copy.wait()
    values = jnp.dot(context, up_ref[...], preferred_element_type=F32).astype(BF)
    picked = jnp.dot((first == target).astype(BF), values, preferred_element_type=F32).astype(BF)
    summed = jnp.dot(picked, out_ref[...], preferred_element_type=F32).astype(BF)
    groups, per_group, _ = sum_ref.shape
    for e in range(groups):
        sum_ref[e] = summed[e * per_group : (e + 1) * per_group]


def normed(states, gain):
    scale = lax.rsqrt(jnp.mean(states * states, axis=-1, keepdims=True) + 1e-06)
    return (states * scale * gain).astype(BF)


def far_sum_kernel(parts_ref, residual_ref, out_ref):
    total = parts_ref[0].astype(F32)
    for e in range(1, parts_ref.shape[0]):
        total = total + parts_ref[e].astype(F32)
    residual = residual_ref[...].astype(F32)
    rows = residual.shape[0]
    near = lax.rem(lax.axis_index("expert"), NEAR)
    twice = jnp.concatenate([residual] * NEAR, axis=0)
    place = lax.broadcasted_iota(jnp.int32, twice.shape, 0) // rows
    out_ref[...] = (total + jnp.where(place == near, twice, 0.0)).astype(BF)


def norm_draft_kernel(mine_ref, theirs_ref, gain_ref, out_ref):
    states = mine_ref[...].astype(F32) + theirs_ref[...].astype(F32)
    tokens = normed(states, gain_ref[...])
    for c in range(out_ref.shape[0]):
        out_ref[c] = tokens


def expert_kernel(codes, draft_ref, draft_other_ref, verify_ref, verify_other_ref, gain_ref, weight_hbm, out_ref,
                  weight_ref, tokens_ref, semaphores):
    chunks = semaphores.shape[0]
    depth = weight_ref.shape[0] // chunks
    copies = [
        pltpu.make_async_copy(
            weight_hbm.at[pl.ds(i * depth, depth)], weight_ref.at[pl.ds(i * depth, depth)], semaphores.at[i]
        )
        for i in range(chunks)
    ]
    for copy in copies:
        copy.start()
    n_dp = lax.axis_size("dp")
    dp = lax.axis_index("dp")
    me = lax.axis_index("expert") * n_dp + dp
    groups, per_group, width = draft_ref.shape
    per = out_ref.shape[2]
    rows = groups * per_group
    tokens_ref[:rows] = draft_ref[...].reshape(rows, width)
    tokens_ref[rows : 2 * rows] = draft_other_ref[...].reshape(rows, width)
    gain = gain_ref[...].astype(F32)
    half = verify_ref.shape[0]
    for part, states_ref in enumerate((verify_ref, verify_other_ref)):
        for start in range(0, half, ROW_BLOCK):
            stop = min(start + ROW_BLOCK, half)
            place = 2 * rows + part * half
            tokens_ref[place + start : place + stop] = normed(states_ref[start:stop].astype(F32), gain)
    total = tokens_ref.shape[0]
    for first in range(0, total, ROW_BLOCK):
        last = min(first + ROW_BLOCK, total)
        product = 0.0
        for i, copy in enumerate(copies):
            if first == 0:
                copy.wait()
            part = slice(i * depth, (i + 1) * depth)
            product = product + jnp.dot(
                tokens_ref[first:last, part], weight_ref[part], preferred_element_type=F32
            )
        active = (product * jax.nn.sigmoid(product)).astype(BF)
        for unit in range(first // per, last // per):
            if unit * per < 2 * rows:
                part, e = divmod(unit, rows // per)
                target, t = n_dp * e + (dp ^ part), 0
            else:
                block, t = divmod(unit - 2 * rows // per, VERIFY - 1)
                target, t = me ^ codes[block], t + 1
            out_ref[target, t] = active[unit * per - first : unit * per - first + per]


def select_kernel(ids_ref, gates_ref, back_ref, out_ref):
    devices, _, per, _ = back_ref.shape
    top = ids_ref.shape[2]
    eye = lax.broadcasted_iota(jnp.int32, (top, top), 0) == lax.broadcasted_iota(
        jnp.int32, (top, top), 1
    )
    source = lax.broadcasted_iota(jnp.int32, (top, devices), 1)
    for t in range(ids_ref.shape[0]):
        for q in range(ids_ref.shape[1]):
            ids = jnp.sum(jnp.where(eye, ids_ref[t, q : q + 1, :], 0), axis=1, keepdims=True)
            gates = jnp.sum(
                jnp.where(eye, gates_ref[t, q : q + 1, :], 0.0), axis=1, keepdims=True
            )
            chosen = (ids == source).astype(BF)
            place = q if t == 0 else per + q * (VERIFY - 1) + t - 1
            rows = back_ref[:, place // per, place % per, :]
            active = jnp.dot(chosen, rows, preferred_element_type=F32)
            out_ref[q, t] = (gates * active).astype(BF)


def swap(x, axis, size, mask):
    return lax.ppermute(x, axis, [(i, i ^ mask) for i in range(size)])


def local_call(kernel, name, outs, *args, hbm=(), scratch=(), mib=24, flops=10**9):
    return pl.pallas_call(
        kernel,
        out_shape=outs,
        in_specs=[HBM if i in hbm else VMEM for i in range(len(args))],
        out_specs=jax.tree.map(lambda _: VMEM, outs),
        scratch_shapes=scratch,
        name=name,
        compiler_params=params(mib),
        cost_estimate=pl.CostEstimate(flops=flops, bytes_accessed=1, transcendentals=0),
    )(*args)


def fetched(*args):
    return tuple(pltpu.VMEM(x.shape, x.dtype) for x in args) + (
        pltpu.SemaphoreType.DMA((len(args),)),
    )


def after(x, other):
    return lax.optimization_barrier((x, other))[0]


def per_device(queries, kv_pages, page_tables, lengths, owners, up_values, out_proj, residual,
               verify_states, norm_gain, route_ids, route_weights, expert_up):
    rows, _, key_width = queries.shape
    verify_rows, width = residual.shape
    n_expert, n_dp = lax.axis_size("expert"), lax.axis_size("dp")
    experts = n_expert * n_dp
    hidden = expert_up.shape[2]
    far = n_expert // NEAR
    far_groups = [[f * NEAR + n for f in range(far)] for n in range(NEAR)]
    shape = jax.ShapeDtypeStruct

    operands = (
        queries.reshape(rows, key_width),
        kv_pages.reshape(-1, key_width),
        page_tables.T,
        lengths.reshape(1, rows),
        owners.reshape(1, rows),
        up_values[0],
        out_proj[0],
    )
    partial_sums = local_call(
        functools.partial(attention_kernel, verify_rows),
        "attention",
        shape((far, NEAR * verify_rows, width), BF),
        *operands,
        hbm=range(7),
        scratch=fetched(*operands),
        mib=60,
        flops=4 * 10**9,
    )
    parts = lax.all_to_all(
        partial_sums, "expert", split_axis=0, concat_axis=0, tiled=True,
        axis_index_groups=far_groups,
    )
    near_sum = local_call(
        far_sum_kernel, "far_sum", shape((NEAR * verify_rows, width), BF), parts, residual
    )
    tokens = local_call(
        norm_draft_kernel,
        "norm_draft",
        shape((far, NEAR * verify_rows, width), BF),
        near_sum,
        swap(near_sum, "expert", n_expert, 1),
        after(norm_gain, partial_sums).reshape(1, width),
    )
    draft = lax.all_to_all(
        tokens, "expert", split_axis=0, concat_axis=0, tiled=True, axis_index_groups=far_groups
    )

    masks = [n_expert // 2] + [1 << i for i in range(n_expert.bit_length() - 2)]
    gathered, codes = verify_states.reshape(-1, width), [0]
    other = swap(verify_states, "expert", n_expert, masks[0]).reshape(-1, width)
    for step, mask in enumerate(masks):
        if step:
            gathered = after(gathered, partial_sums if step < len(masks) - 1 else near_sum)
            other = swap(gathered, "expert", n_expert, mask)
        gathered = jnp.concatenate([gathered, other], axis=0)
        codes += [code ^ (mask * n_dp) for code in codes]
    gathered_other = swap(after(gathered, tokens), "dp", n_dp, 1)
    codes += [code ^ 1 for code in codes]
    token_rows = experts * verify_rows * VERIFY
    active = local_call(
        functools.partial(expert_kernel, codes),
        "expert",
        shape((experts, VERIFY, verify_rows, hidden), BF),
        draft, swap(draft, "dp", n_dp, 1), gathered, gathered_other,
        after(norm_gain, partial_sums).reshape(1, width), expert_up[0],
        hbm=(5,),
        scratch=(
            pltpu.VMEM((width, hidden), BF),
            pltpu.VMEM((token_rows, width), BF),
            pltpu.SemaphoreType.DMA((CHUNKS,)),
        ),
        mib=52,
        flops=4 * 10**9,
    )
    back = lax.all_to_all(active, ("expert", "dp"), split_axis=0, concat_axis=0, tiled=True)
    return local_call(
        select_kernel,
        "select",
        shape((verify_rows, VERIFY, route_ids.shape[2], hidden), BF),
        route_ids.transpose(1, 0, 2), route_weights.transpose(1, 0, 2), back,
    )


def solution(mesh):
    placed = (
        P(("groups", "dp"), "expert", None),
        P(("groups", "dp"), None, None),
        P(("groups", "dp"), None),
        P(("groups", "dp")),
        P(("groups", "dp")),
        P("expert", None, None),
        P("expert", None, None),
        P(("groups", "expert", "dp"), None),
        P(("groups", "expert", "dp"), None, None),
        P(),
        P(("groups", "expert", "dp"), None, None),
        P(("groups", "expert", "dp"), None, None),
        P(("expert", "dp"), None, None),
    )
    return jax.shard_map(
        per_device,
        mesh=mesh,
        in_specs=placed,
        out_specs=P(("groups", "expert", "dp"), None, None, None),
        check_vma=False,
    )
```

```python
import functools

import jax
import jax.numpy as jnp
from jax import lax
from jax.experimental import pallas as pl
from jax.experimental.pallas import tpu as pltpu
from jax.sharding import PartitionSpec as P

LATENT = 512
ROPE = 64
VHEAD = 128
VERIFY = 3
PAGES = 32
NEAR = 2
CHUNKS = 7
KV_CHUNKS = 4
ROW_BLOCK = 256
BF = jnp.bfloat16
F32 = jnp.float32
VMEM = pl.BlockSpec(memory_space=pltpu.VMEM)
HBM = pl.BlockSpec(memory_space=pltpu.HBM)


def params(mib=40):
    return pltpu.CompilerParams(vmem_limit_bytes=mib * 1024 * 1024)


def as_column(row, size):
    eye = lax.broadcasted_iota(jnp.int32, (size, size), 0) == lax.broadcasted_iota(
        jnp.int32, (size, size), 1
    )
    return jnp.sum(jnp.where(eye, row, 0), axis=1, keepdims=True)


def fetch(sources, targets, semaphores):
    copies = [
        pltpu.make_async_copy(source, target, semaphores.at[i])
        for i, (source, target) in enumerate(zip(sources, targets))
    ]
    for copy in copies:
        copy.start()
    return copies


def attention_kernel(per_owner, *refs):
    sources, sum_ref, targets, semaphores = refs[:7], refs[7], refs[8:15], refs[15]
    table_ref, length_ref, owner_ref, q_ref, up_ref, out_ref, kv_ref = targets
    small = fetch(sources[:4], targets[:4], semaphores)
    part = kv_ref.shape[0] // KV_CHUNKS
    chunks = [
        pltpu.make_async_copy(
            sources[6].at[pl.ds(i * part, part)], kv_ref.at[pl.ds(i * part, part)], semaphores.at[6 + i]
        )
        for i in range(KV_CHUNKS)
    ]
    for copy in chunks:
        copy.start()
    weights = fetch(sources[4:6], targets[4:6], semaphores.at[pl.ds(4, 2)])
    rows = q_ref.shape[0]
    tokens = kv_ref.shape[0]
    slots = table_ref.shape[0]
    page_len = tokens // PAGES
    token = lax.broadcasted_iota(jnp.int32, (1, tokens), 1)
    page, offset = token // page_len, token % page_len
    position = jnp.full((rows, tokens), 1 << 24, jnp.int32)
    for copy in small:
        copy.wait()
    for slot in range(slots):
        named = as_column(table_ref[slot : slot + 1, :], rows)
        position = jnp.where(named == page, slot * page_len + offset, position)
    visible = position < as_column(length_ref[...], rows)
    owner = owner_ref[...]
    first = lax.broadcasted_iota(jnp.int32, (rows, rows), 0)
    second = lax.broadcasted_iota(jnp.int32, (rows, rows), 1)
    before = (as_column(owner, rows) == owner) & (first < second)
    target = owner * per_owner + jnp.sum(before.astype(jnp.int32), axis=0, keepdims=True)
    scores = []
    for i, copy in enumerate(chunks):
        copy.wait()
        scores.append(
            lax.dot_general(
                q_ref[...],
                kv_ref[i * part : (i + 1) * part],
                (((1,), (1,)), ((), ())),
                preferred_element_type=F32,
            )
        )
    scores = jnp.concatenate(scores, axis=1) * (VHEAD + ROPE) ** (-0.5)
    masked = jnp.where(visible, scores, -1e30)
    row_max = jnp.max(masked, axis=1, keepdims=True)
    exponent = jnp.where(visible, jnp.exp(masked - row_max), 0.0)
    attention = (exponent / jnp.sum(exponent, axis=1, keepdims=True)).astype(BF)
    context = jnp.dot(attention, kv_ref[:, :LATENT], preferred_element_type=F32).astype(BF)
    for copy in weights:
        copy.wait()
    values = jnp.dot(context, up_ref[...], preferred_element_type=F32).astype(BF)
    picked = jnp.dot((first == target).astype(BF), values, preferred_element_type=F32).astype(BF)
    summed = jnp.dot(picked, out_ref[...], preferred_element_type=F32).astype(BF)
    groups, per_group, _ = sum_ref.shape
    for e in range(groups):
        sum_ref[e] = summed[e * per_group : (e + 1) * per_group]


def normed(states, gain):
    scale = lax.rsqrt(jnp.mean(states * states, axis=-1, keepdims=True) + 1e-06)
    return (states * scale * gain).astype(BF)


def far_sum_kernel(parts_ref, residual_ref, out_ref):
    total = parts_ref[0].astype(F32)
    for e in range(1, parts_ref.shape[0]):
        total = total + parts_ref[e].astype(F32)
    residual = residual_ref[...].astype(F32)
    rows = residual.shape[0]
    near = lax.rem(lax.axis_index("expert"), NEAR)
    twice = jnp.concatenate([residual] * NEAR, axis=0)
    place = lax.broadcasted_iota(jnp.int32, twice.shape, 0) // rows
    out_ref[...] = (total + jnp.where(place == near, twice, 0.0)).astype(BF)


def norm_draft_kernel(mine_ref, theirs_ref, gain_ref, out_ref):
    states = mine_ref[...].astype(F32) + theirs_ref[...].astype(F32)
    tokens = normed(states, gain_ref[...])
    for c in range(out_ref.shape[0]):
        out_ref[c] = tokens


def expert_kernel(codes, draft_ref, draft_other_ref, verify_ref, verify_other_ref, gain_ref, weight_hbm, out_ref,
                  weight_ref, tokens_ref, semaphores):
    chunks = semaphores.shape[0]
    depth = weight_ref.shape[0] // chunks
    copies = [
        pltpu.make_async_copy(
            weight_hbm.at[pl.ds(i * depth, depth)], weight_ref.at[pl.ds(i * depth, depth)], semaphores.at[i]
        )
        for i in range(chunks)
    ]
    for copy in copies:
        copy.start()
    n_dp = lax.axis_size("dp")
    dp = lax.axis_index("dp")
    me = lax.axis_index("expert") * n_dp + dp
    groups, per_group, width = draft_ref.shape
    per = out_ref.shape[2]
    rows = groups * per_group
    tokens_ref[:rows] = draft_ref[...].reshape(rows, width)
    tokens_ref[rows : 2 * rows] = draft_other_ref[...].reshape(rows, width)
    gain = gain_ref[...].astype(F32)
    half = verify_ref.shape[0]
    for part, states_ref in enumerate((verify_ref, verify_other_ref)):
        for start in range(0, half, ROW_BLOCK):
            stop = min(start + ROW_BLOCK, half)
            place = 2 * rows + part * half
            tokens_ref[place + start : place + stop] = normed(states_ref[start:stop].astype(F32), gain)
    total = tokens_ref.shape[0]
    for first in range(0, total, ROW_BLOCK):
        last = min(first + ROW_BLOCK, total)
        product = 0.0
        for i, copy in enumerate(copies):
            if first == 0:
                copy.wait()
            part = slice(i * depth, (i + 1) * depth)
            product = product + jnp.dot(
                tokens_ref[first:last, part], weight_ref[part], preferred_element_type=F32
            )
        active = (product * jax.nn.sigmoid(product)).astype(BF)
        for unit in range(first // per, last // per):
            if unit * per < 2 * rows:
                part, e = divmod(unit, rows // per)
                target, t = n_dp * e + (dp ^ part), 0
            else:
                block, t = divmod(unit - 2 * rows // per, VERIFY - 1)
                target, t = me ^ codes[block], t + 1
            out_ref[target, t] = active[unit * per - first : unit * per - first + per]


def select_kernel(ids_ref, gates_ref, back_ref, out_ref):
    devices, groups, per, width = back_ref.shape
    top = ids_ref.shape[2]
    eye = lax.broadcasted_iota(jnp.int32, (top, top), 0) == lax.broadcasted_iota(
        jnp.int32, (top, top), 1
    )
    source = lax.broadcasted_iota(jnp.int32, (top, devices * per), 1)
    for group in range(groups):
        places, chosen, gates = [], [], []
        for r in range(per):
            if group == 0:
                q, t = r, 0
            else:
                q, t = divmod((group - 1) * per + r, VERIFY - 1)
                t += 1
            ids = jnp.sum(jnp.where(eye, ids_ref[t, q : q + 1, :], 0), axis=1, keepdims=True)
            gates.append(
                jnp.sum(jnp.where(eye, gates_ref[t, q : q + 1, :], 0.0), axis=1, keepdims=True)
            )
            chosen.append((ids * per + r == source).astype(F32))
            places.append((q, t))
        rows = back_ref[:, group].reshape(devices * per, width)
        active = jnp.dot(
            jnp.concatenate(chosen, axis=0).astype(BF), rows, preferred_element_type=F32
        )
        for r, (q, t) in enumerate(places):
            out_ref[q, t] = (gates[r] * active[r * top : (r + 1) * top]).astype(BF)


def swap(x, axis, size, mask):
    return lax.ppermute(x, axis, [(i, i ^ mask) for i in range(size)])


def local_call(kernel, name, outs, *args, hbm=(), scratch=(), mib=24, flops=10**9):
    return pl.pallas_call(
        kernel,
        out_shape=outs,
        in_specs=[HBM if i in hbm else VMEM for i in range(len(args))],
        out_specs=jax.tree.map(lambda _: VMEM, outs),
        scratch_shapes=scratch,
        name=name,
        compiler_params=params(mib),
        cost_estimate=pl.CostEstimate(flops=flops, bytes_accessed=1, transcendentals=0),
    )(*args)


def fetched(*args, more=0):
    return tuple(pltpu.VMEM(x.shape, x.dtype) for x in args) + (
        pltpu.SemaphoreType.DMA((len(args) + more,)),
    )


def after(x, other):
    return lax.optimization_barrier((x, other))[0]


def per_device(queries, kv_pages, page_tables, lengths, owners, up_values, out_proj, residual,
               verify_states, norm_gain, route_ids, route_weights, expert_up):
    rows, _, key_width = queries.shape
    verify_rows, width = residual.shape
    n_expert, n_dp = lax.axis_size("expert"), lax.axis_size("dp")
    experts = n_expert * n_dp
    hidden = expert_up.shape[2]
    far = n_expert // NEAR
    far_groups = [[f * NEAR + n for f in range(far)] for n in range(NEAR)]
    shape = jax.ShapeDtypeStruct

    operands = (
        page_tables.T,
        lengths.reshape(1, rows),
        owners.reshape(1, rows),
        queries.reshape(rows, key_width),
        up_values[0],
        out_proj[0],
        kv_pages.reshape(-1, key_width),
    )
    partial_sums = local_call(
        functools.partial(attention_kernel, verify_rows),
        "attention",
        shape((far, NEAR * verify_rows, width), BF),
        *operands,
        hbm=range(7),
        scratch=fetched(*operands, more=KV_CHUNKS - 1),
        mib=60,
        flops=4000000000,
    )
    parts = lax.all_to_all(
        partial_sums, "expert", split_axis=0, concat_axis=0, tiled=True,
        axis_index_groups=far_groups,
    )
    near_sum = local_call(
        far_sum_kernel, "far_sum", shape((NEAR * verify_rows, width), BF), parts, residual, flops=1000000000,
    )
    tokens = local_call(
        norm_draft_kernel,
        "norm_draft",
        shape((far, NEAR * verify_rows, width), BF),
        near_sum,
        swap(near_sum, "expert", n_expert, 1),
        after(norm_gain, partial_sums).reshape(1, width),
    )
    draft = lax.all_to_all(
        tokens, "expert", split_axis=0, concat_axis=0, tiled=True, axis_index_groups=far_groups
    )

    masks = [n_expert // 2] + [1 << i for i in range(n_expert.bit_length() - 2)]
    gathered, codes = verify_states.reshape(-1, width), [0]
    other = swap(verify_states, "expert", n_expert, masks[0]).reshape(-1, width)
    for step, mask in enumerate(masks):
        if step:
            other = swap(gathered, "expert", n_expert, mask)
        if step < len(masks) - 2:
            gathered = gathered
        elif step < len(masks) - 1:
            gathered = after(gathered, near_sum)
        else:
            gathered = after(gathered, tokens)
        gathered = jnp.concatenate([gathered, other], axis=0)
        codes += [code ^ (mask * n_dp) for code in codes]
    gathered_other = swap(gathered, "dp", n_dp, 1)
    codes += [code ^ 1 for code in codes]
    token_rows = experts * verify_rows * VERIFY
    active = local_call(
        functools.partial(expert_kernel, codes),
        "expert",
        shape((experts, VERIFY, verify_rows, hidden), BF),
        draft, swap(draft, "dp", n_dp, 1), gathered, gathered_other,
        after(norm_gain, partial_sums).reshape(1, width), expert_up[0],
        hbm=(5,),
        scratch=(
            pltpu.VMEM((width, hidden), BF),
            pltpu.VMEM((token_rows, width), BF),
            pltpu.SemaphoreType.DMA((CHUNKS,)),
        ),
        mib=52,
        flops=4 * 10**9,
    )
    back = lax.all_to_all(active, ("expert", "dp"), split_axis=0, concat_axis=0, tiled=True)
    return local_call(
        select_kernel,
        "select",
        shape((verify_rows, VERIFY, route_ids.shape[2], hidden), BF),
        route_ids.transpose(1, 0, 2), route_weights.transpose(1, 0, 2), back,
    )


def solution(mesh):
    placed = (
        P(("groups", "dp"), "expert", None),
        P(("groups", "dp"), None, None),
        P(("groups", "dp"), None),
        P(("groups", "dp")),
        P(("groups", "dp")),
        P("expert", None, None),
        P("expert", None, None),
        P(("groups", "expert", "dp"), None),
        P(("groups", "expert", "dp"), None, None),
        P(),
        P(("groups", "expert", "dp"), None, None),
        P(("groups", "expert", "dp"), None, None),
        P(("expert", "dp"), None, None),
    )
    return jax.shard_map(
        per_device,
        mesh=mesh,
        in_specs=placed,
        out_specs=P(("groups", "expert", "dp"), None, None, None),
        check_vma=False,
    )
```

```python
import functools

import jax
import jax.numpy as jnp
from jax import lax
from jax.experimental import pallas as pl
from jax.experimental.pallas import tpu as pltpu
from jax.sharding import PartitionSpec as P

LATENT = 512
ROPE = 64
VHEAD = 128
VERIFY = 3
PAGES = 32
NEAR = 2
CHUNKS = 4
KV_CHUNKS = 2
ROW_BLOCK = 256
BF = jnp.bfloat16
F32 = jnp.float32
VMEM = pl.BlockSpec(memory_space=pltpu.VMEM)
HBM = pl.BlockSpec(memory_space=pltpu.HBM)


def params(mib=40):
    return pltpu.CompilerParams(vmem_limit_bytes=mib * 1024 * 1024)


def as_column(row, size):
    eye = lax.broadcasted_iota(jnp.int32, (size, size), 0) == lax.broadcasted_iota(
        jnp.int32, (size, size), 1
    )
    return jnp.sum(jnp.where(eye, row, 0), axis=1, keepdims=True)


def fetch(sources, targets, semaphores):
    copies = [
        pltpu.make_async_copy(source, target, semaphores.at[i])
        for i, (source, target) in enumerate(zip(sources, targets))
    ]
    for copy in copies:
        copy.start()
    return copies


def attention_kernel(per_owner, *refs):
    sources, sum_ref, targets, semaphores = refs[:7], refs[7], refs[8:15], refs[15]
    table_ref, length_ref, owner_ref, q_ref, up_ref, out_ref, kv_ref = targets
    small = fetch(sources[:4], targets[:4], semaphores)
    part = kv_ref.shape[0] // KV_CHUNKS
    chunks = [
        pltpu.make_async_copy(
            sources[6].at[pl.ds(i * part, part)], kv_ref.at[pl.ds(i * part, part)], semaphores.at[6 + i]
        )
        for i in range(KV_CHUNKS)
    ]
    for copy in chunks:
        copy.start()
    weights = fetch(sources[4:6], targets[4:6], semaphores.at[pl.ds(4, 2)])
    rows = q_ref.shape[0]
    tokens = kv_ref.shape[0]
    slots = table_ref.shape[0]
    page_len = tokens // PAGES
    token = lax.broadcasted_iota(jnp.int32, (1, tokens), 1)
    page, offset = token // page_len, token % page_len
    position = jnp.full((rows, tokens), 1 << 24, jnp.int32)
    for copy in small:
        copy.wait()
    for slot in range(slots):
        named = as_column(table_ref[slot : slot + 1, :], rows)
        position = jnp.where(named == page, slot * page_len + offset, position)
    visible = position < as_column(length_ref[...], rows)
    owner = owner_ref[...]
    first = lax.broadcasted_iota(jnp.int32, (rows, rows), 0)
    second = lax.broadcasted_iota(jnp.int32, (rows, rows), 1)
    before = (as_column(owner, rows) == owner) & (first < second)
    target = owner * per_owner + jnp.sum(before.astype(jnp.int32), axis=0, keepdims=True)
    scores = []
    for i, copy in enumerate(chunks):
        copy.wait()
        scores.append(
            lax.dot_general(
                q_ref[...],
                kv_ref[i * part : (i + 1) * part],
                (((1,), (1,)), ((), ())),
                preferred_element_type=F32,
            )
        )
    scores = jnp.concatenate(scores, axis=1) * (VHEAD + ROPE) ** (-0.5)
    masked = jnp.where(visible, scores, -1e30)
    row_max = jnp.max(masked, axis=1, keepdims=True)
    exponent = jnp.where(visible, jnp.exp(masked - row_max), 0.0)
    attention = (exponent / jnp.sum(exponent, axis=1, keepdims=True)).astype(BF)
    context = jnp.dot(attention, kv_ref[:, :LATENT], preferred_element_type=F32).astype(BF)
    for copy in weights:
        copy.wait()
    values = jnp.dot(context, up_ref[...], preferred_element_type=F32).astype(BF)
    picked = jnp.dot((first == target).astype(BF), values, preferred_element_type=F32).astype(BF)
    summed = jnp.dot(picked, out_ref[...], preferred_element_type=F32).astype(BF)
    groups, per_group, _ = sum_ref.shape
    for e in range(groups):
        sum_ref[e] = summed[e * per_group : (e + 1) * per_group]


def normed(states, gain):
    scale = lax.rsqrt(jnp.mean(states * states, axis=-1, keepdims=True) + 1e-06)
    return (states * scale * gain).astype(BF)


def far_sum_kernel(parts_ref, residual_ref, out_ref):
    total = parts_ref[0].astype(F32)
    for e in range(1, parts_ref.shape[0]):
        total = total + parts_ref[e].astype(F32)
    residual = residual_ref[...].astype(F32)
    rows = residual.shape[0]
    near = lax.rem(lax.axis_index("expert"), NEAR)
    twice = jnp.concatenate([residual] * NEAR, axis=0)
    place = lax.broadcasted_iota(jnp.int32, twice.shape, 0) // rows
    out_ref[...] = (total + jnp.where(place == near, twice, 0.0)).astype(BF)


def norm_draft_kernel(mine_ref, theirs_ref, gain_ref, out_ref):
    states = mine_ref[...].astype(F32) + theirs_ref[...].astype(F32)
    tokens = normed(states, gain_ref[...])
    for c in range(out_ref.shape[0]):
        out_ref[c] = tokens


def expert_kernel(codes, draft_ref, draft_other_ref, verify_ref, verify_other_ref, gain_ref, weight_hbm, out_ref,
                  weight_ref, tokens_ref, semaphores):
    chunks = semaphores.shape[0]
    depth = weight_ref.shape[0] // chunks
    copies = [
        pltpu.make_async_copy(
            weight_hbm.at[pl.ds(i * depth, depth)], weight_ref.at[pl.ds(i * depth, depth)], semaphores.at[i]
        )
        for i in range(chunks)
    ]
    for copy in copies:
        copy.start()
    n_dp = lax.axis_size("dp")
    dp = lax.axis_index("dp")
    me = lax.axis_index("expert") * n_dp + dp
    groups, per_group, width = draft_ref.shape
    per = out_ref.shape[2]
    rows = groups * per_group
    tokens_ref[:rows] = draft_ref[...].reshape(rows, width)
    tokens_ref[rows : 2 * rows] = draft_other_ref[...].reshape(rows, width)
    gain = gain_ref[...].astype(F32)
    half = verify_ref.shape[0]
    for part, states_ref in enumerate((verify_ref, verify_other_ref)):
        for start in range(0, half, ROW_BLOCK):
            stop = min(start + ROW_BLOCK, half)
            place = 2 * rows + part * half
            tokens_ref[place + start : place + stop] = normed(states_ref[start:stop].astype(F32), gain)
    total = tokens_ref.shape[0]
    for first in range(0, total, ROW_BLOCK):
        last = min(first + ROW_BLOCK, total)
        product = 0.0
        for i, copy in enumerate(copies):
            if first == 0:
                copy.wait()
            part = slice(i * depth, (i + 1) * depth)
            product = product + jnp.dot(
                tokens_ref[first:last, part], weight_ref[part], preferred_element_type=F32
            )
        active = (product * jax.nn.sigmoid(product)).astype(BF)
        for unit in range(first // per, last // per):
            if unit * per < 2 * rows:
                part, e = divmod(unit, rows // per)
                target, t = n_dp * e + (dp ^ part), 0
            else:
                block, t = divmod(unit - 2 * rows // per, VERIFY - 1)
                target, t = me ^ codes[block], t + 1
            out_ref[target, t] = active[unit * per - first : unit * per - first + per]


def select_kernel(ids_ref, gates_ref, back_ref, out_ref):
    devices, groups, per, width = back_ref.shape
    top = ids_ref.shape[2]
    eye = lax.broadcasted_iota(jnp.int32, (top, top), 0) == lax.broadcasted_iota(
        jnp.int32, (top, top), 1
    )
    source = lax.broadcasted_iota(jnp.int32, (top, devices * per), 1)
    for group in range(groups):
        places, chosen, gates = [], [], []
        for r in range(per):
            if group == 0:
                q, t = r, 0
            else:
                q, t = divmod((group - 1) * per + r, VERIFY - 1)
                t += 1
            ids = jnp.sum(jnp.where(eye, ids_ref[t, q : q + 1, :], 0), axis=1, keepdims=True)
            gates.append(
                jnp.sum(jnp.where(eye, gates_ref[t, q : q + 1, :], 0.0), axis=1, keepdims=True)
            )
            chosen.append((ids * per + r == source).astype(F32))
            places.append((q, t))
        rows = back_ref[:, group].reshape(devices * per, width)
        active = jnp.dot(
            jnp.concatenate(chosen, axis=0).astype(BF), rows, preferred_element_type=F32
        )
        for r, (q, t) in enumerate(places):
            out_ref[q, t] = (gates[r] * active[r * top : (r + 1) * top]).astype(BF)


def swap(x, axis, size, mask):
    return lax.ppermute(x, axis, [(i, i ^ mask) for i in range(size)])


def local_call(kernel, name, outs, *args, hbm=(), scratch=(), mib=24, flops=10**9):
    return pl.pallas_call(
        kernel,
        out_shape=outs,
        in_specs=[HBM if i in hbm else VMEM for i in range(len(args))],
        out_specs=jax.tree.map(lambda _: VMEM, outs),
        scratch_shapes=scratch,
        name=name,
        compiler_params=params(mib),
        cost_estimate=pl.CostEstimate(flops=flops, bytes_accessed=1, transcendentals=0),
    )(*args)


def fetched(*args, more=0):
    return tuple(pltpu.VMEM(x.shape, x.dtype) for x in args) + (
        pltpu.SemaphoreType.DMA((len(args) + more,)),
    )


def after(x, other):
    return lax.optimization_barrier((x, other))[0]


def per_device(queries, kv_pages, page_tables, lengths, owners, up_values, out_proj, residual,
               verify_states, norm_gain, route_ids, route_weights, expert_up):
    rows, _, key_width = queries.shape
    verify_rows, width = residual.shape
    n_expert, n_dp = lax.axis_size("expert"), lax.axis_size("dp")
    experts = n_expert * n_dp
    hidden = expert_up.shape[2]
    far = n_expert // NEAR
    far_groups = [[f * NEAR + n for f in range(far)] for n in range(NEAR)]
    shape = jax.ShapeDtypeStruct

    operands = (
        page_tables.T,
        lengths.reshape(1, rows),
        owners.reshape(1, rows),
        queries.reshape(rows, key_width),
        up_values[0],
        out_proj[0],
        kv_pages.reshape(-1, key_width),
    )
    partial_sums = local_call(
        functools.partial(attention_kernel, verify_rows),
        "attention",
        shape((far, NEAR * verify_rows, width), BF),
        *operands,
        hbm=range(7),
        scratch=fetched(*operands, more=KV_CHUNKS - 1),
        mib=60,
        flops=4000000000,
    )
    parts = lax.all_to_all(
        partial_sums, "expert", split_axis=0, concat_axis=0, tiled=True,
        axis_index_groups=far_groups,
    )
    near_sum = local_call(
        far_sum_kernel, "far_sum", shape((NEAR * verify_rows, width), BF), parts, residual, flops=1000000000,
    )
    tokens = local_call(
        norm_draft_kernel,
        "norm_draft",
        shape((far, NEAR * verify_rows, width), BF),
        near_sum,
        swap(near_sum, "expert", n_expert, 1),
        after(norm_gain, partial_sums).reshape(1, width),
    )
    draft = lax.all_to_all(
        tokens, "expert", split_axis=0, concat_axis=0, tiled=True, axis_index_groups=far_groups
    )

    masks = [n_expert // 2] + [1 << i for i in range(n_expert.bit_length() - 2)]
    gathered, codes = verify_states.reshape(-1, width), [0]
    other = swap(verify_states, "expert", n_expert, masks[0]).reshape(-1, width)
    for step, mask in enumerate(masks):
        if step:
            other = swap(gathered, "expert", n_expert, mask)
        if step < len(masks) - 2:
            gathered = gathered
        elif step < len(masks) - 1:
            gathered = after(gathered, near_sum)
        else:
            gathered = after(gathered, tokens)
        gathered = jnp.concatenate([gathered, other], axis=0)
        codes += [code ^ (mask * n_dp) for code in codes]
    gathered_other = swap(gathered, "dp", n_dp, 1)
    codes += [code ^ 1 for code in codes]
    token_rows = experts * verify_rows * VERIFY
    active = local_call(
        functools.partial(expert_kernel, codes),
        "expert",
        shape((experts, VERIFY, verify_rows, hidden), BF),
        draft, swap(draft, "dp", n_dp, 1), gathered, gathered_other,
        after(norm_gain, partial_sums).reshape(1, width), expert_up[0],
        hbm=(5,),
        scratch=(
            pltpu.VMEM((width, hidden), BF),
            pltpu.VMEM((token_rows, width), BF),
            pltpu.SemaphoreType.DMA((CHUNKS,)),
        ),
        mib=52,
        flops=4 * 10**9,
    )
    back = lax.all_to_all(active, ("expert", "dp"), split_axis=0, concat_axis=0, tiled=True)
    return local_call(
        select_kernel,
        "select",
        shape((verify_rows, VERIFY, route_ids.shape[2], hidden), BF),
        route_ids.transpose(1, 0, 2), route_weights.transpose(1, 0, 2), back,
    )


def solution(mesh):
    placed = (
        P(("groups", "dp"), "expert", None),
        P(("groups", "dp"), None, None),
        P(("groups", "dp"), None),
        P(("groups", "dp")),
        P(("groups", "dp")),
        P("expert", None, None),
        P("expert", None, None),
        P(("groups", "expert", "dp"), None),
        P(("groups", "expert", "dp"), None, None),
        P(),
        P(("groups", "expert", "dp"), None, None),
        P(("groups", "expert", "dp"), None, None),
        P(("expert", "dp"), None, None),
    )
    return jax.shard_map(
        per_device,
        mesh=mesh,
        in_specs=placed,
        out_specs=P(("groups", "expert", "dp"), None, None, None),
        check_vma=False,
    )
```

```python
import functools

import jax
import jax.numpy as jnp
from jax import lax
from jax.experimental import pallas as pl
from jax.experimental.pallas import tpu as pltpu
from jax.sharding import PartitionSpec as P

LATENT = 512
ROPE = 64
VHEAD = 128
VERIFY = 3
PAGES = 32
NEAR = 2
CHUNKS = 7
KV_CHUNKS = 2
ROW_BLOCK = 256
BF = jnp.bfloat16
F32 = jnp.float32
VMEM = pl.BlockSpec(memory_space=pltpu.VMEM)
HBM = pl.BlockSpec(memory_space=pltpu.HBM)


def params(mib=40):
    return pltpu.CompilerParams(vmem_limit_bytes=mib * 1024 * 1024)


def as_column(row, size):
    eye = lax.broadcasted_iota(jnp.int32, (size, size), 0) == lax.broadcasted_iota(
        jnp.int32, (size, size), 1
    )
    return jnp.sum(jnp.where(eye, row, 0), axis=1, keepdims=True)


def fetch(sources, targets, semaphores):
    copies = [
        pltpu.make_async_copy(source, target, semaphores.at[i])
        for i, (source, target) in enumerate(zip(sources, targets))
    ]
    for copy in copies:
        copy.start()
    return copies


def attention_kernel(per_owner, *refs):
    sources, sum_ref, targets, semaphores = refs[:7], refs[7], refs[8:15], refs[15]
    table_ref, length_ref, owner_ref, q_ref, up_ref, out_ref, kv_ref = targets
    small = fetch(sources[:4], targets[:4], semaphores)
    part = kv_ref.shape[0] // KV_CHUNKS
    chunks = [
        pltpu.make_async_copy(
            sources[6].at[pl.ds(i * part, part)], kv_ref.at[pl.ds(i * part, part)], semaphores.at[6 + i]
        )
        for i in range(KV_CHUNKS)
    ]
    for copy in chunks:
        copy.start()
    weights = fetch(sources[4:6], targets[4:6], semaphores.at[pl.ds(4, 2)])
    rows = q_ref.shape[0]
    tokens = kv_ref.shape[0]
    slots = table_ref.shape[0]
    page_len = tokens // PAGES
    token = lax.broadcasted_iota(jnp.int32, (1, tokens), 1)
    page, offset = token // page_len, token % page_len
    position = jnp.full((rows, tokens), 1 << 24, jnp.int32)
    for copy in small:
        copy.wait()
    for slot in range(slots):
        named = as_column(table_ref[slot : slot + 1, :], rows)
        position = jnp.where(named == page, slot * page_len + offset, position)
    visible = position < as_column(length_ref[...], rows)
    owner = owner_ref[...]
    first = lax.broadcasted_iota(jnp.int32, (rows, rows), 0)
    second = lax.broadcasted_iota(jnp.int32, (rows, rows), 1)
    before = (as_column(owner, rows) == owner) & (first < second)
    target = owner * per_owner + jnp.sum(before.astype(jnp.int32), axis=0, keepdims=True)
    scores = []
    for i, copy in enumerate(chunks):
        copy.wait()
        scores.append(
            lax.dot_general(
                q_ref[...],
                kv_ref[i * part : (i + 1) * part],
                (((1,), (1,)), ((), ())),
                preferred_element_type=F32,
            )
        )
    scores = jnp.concatenate(scores, axis=1) * (VHEAD + ROPE) ** (-0.5)
    masked = jnp.where(visible, scores, -1e30)
    row_max = jnp.max(masked, axis=1, keepdims=True)
    exponent = jnp.where(visible, jnp.exp(masked - row_max), 0.0)
    attention = (exponent / jnp.sum(exponent, axis=1, keepdims=True)).astype(BF)
    context = jnp.dot(attention, kv_ref[:, :LATENT], preferred_element_type=F32).astype(BF)
    for copy in weights:
        copy.wait()
    values = jnp.dot(context, up_ref[...], preferred_element_type=F32).astype(BF)
    picked = jnp.dot((first == target).astype(BF), values, preferred_element_type=F32).astype(BF)
    summed = jnp.dot(picked, out_ref[...], preferred_element_type=F32).astype(BF)
    groups, per_group, _ = sum_ref.shape
    for e in range(groups):
        sum_ref[e] = summed[e * per_group : (e + 1) * per_group]


def normed(states, gain):
    scale = lax.rsqrt(jnp.mean(states * states, axis=-1, keepdims=True) + 1e-06)
    return (states * scale * gain).astype(BF)


def far_sum_kernel(parts_ref, residual_ref, out_ref):
    total = parts_ref[0].astype(F32)
    for e in range(1, parts_ref.shape[0]):
        total = total + parts_ref[e].astype(F32)
    residual = residual_ref[...].astype(F32)
    rows = residual.shape[0]
    near = lax.rem(lax.axis_index("expert"), NEAR)
    twice = jnp.concatenate([residual] * NEAR, axis=0)
    place = lax.broadcasted_iota(jnp.int32, twice.shape, 0) // rows
    out_ref[...] = (total + jnp.where(place == near, twice, 0.0)).astype(BF)


def norm_draft_kernel(mine_ref, theirs_ref, gain_ref, out_ref):
    states = mine_ref[...].astype(F32) + theirs_ref[...].astype(F32)
    tokens = normed(states, gain_ref[...])
    for c in range(out_ref.shape[0]):
        out_ref[c] = tokens


def expert_kernel(codes, draft_ref, draft_other_ref, verify_ref, verify_other_ref, gain_ref, weight_hbm, out_ref,
                  weight_ref, tokens_ref, semaphores):
    chunks = semaphores.shape[0]
    depth = weight_ref.shape[0] // chunks
    copies = [
        pltpu.make_async_copy(
            weight_hbm.at[pl.ds(i * depth, depth)], weight_ref.at[pl.ds(i * depth, depth)], semaphores.at[i]
        )
        for i in range(chunks)
    ]
    for copy in copies:
        copy.start()
    n_dp = lax.axis_size("dp")
    dp = lax.axis_index("dp")
    me = lax.axis_index("expert") * n_dp + dp
    groups, per_group, width = draft_ref.shape
    per = out_ref.shape[2]
    rows = groups * per_group
    tokens_ref[:rows] = draft_ref[...].reshape(rows, width)
    tokens_ref[rows : 2 * rows] = draft_other_ref[...].reshape(rows, width)
    gain = gain_ref[...].astype(F32)
    half = verify_ref.shape[0]
    for part, states_ref in enumerate((verify_ref, verify_other_ref)):
        for start in range(0, half, ROW_BLOCK):
            stop = min(start + ROW_BLOCK, half)
            place = 2 * rows + part * half
            tokens_ref[place + start : place + stop] = normed(states_ref[start:stop].astype(F32), gain)
    total = tokens_ref.shape[0]
    for first in range(0, total, ROW_BLOCK):
        last = min(first + ROW_BLOCK, total)
        product = 0.0
        for i, copy in enumerate(copies):
            if first == 0:
                copy.wait()
            part = slice(i * depth, (i + 1) * depth)
            product = product + jnp.dot(
                tokens_ref[first:last, part], weight_ref[part], preferred_element_type=F32
            )
        active = (product * jax.nn.sigmoid(product)).astype(BF)
        for unit in range(first // per, last // per):
            if unit * per < 2 * rows:
                part, e = divmod(unit, rows // per)
                target, t = n_dp * e + (dp ^ part), 0
            else:
                block, t = divmod(unit - 2 * rows // per, VERIFY - 1)
                target, t = me ^ codes[block], t + 1
            out_ref[target, t] = active[unit * per - first : unit * per - first + per]


def select_kernel(ids_ref, gates_ref, back_ref, out_ref):
    devices, groups, per, width = back_ref.shape
    top = ids_ref.shape[2]
    eye = lax.broadcasted_iota(jnp.int32, (top, top), 0) == lax.broadcasted_iota(
        jnp.int32, (top, top), 1
    )
    source = lax.broadcasted_iota(jnp.int32, (top, devices * per), 1)
    for group in range(groups):
        places, chosen, gates = [], [], []
        for r in range(per):
            if group == 0:
                q, t = r, 0
            else:
                q, t = divmod((group - 1) * per + r, VERIFY - 1)
                t += 1
            ids = jnp.sum(jnp.where(eye, ids_ref[t, q : q + 1, :], 0), axis=1, keepdims=True)
            gates.append(
                jnp.sum(jnp.where(eye, gates_ref[t, q : q + 1, :], 0.0), axis=1, keepdims=True)
            )
            chosen.append((ids * per + r == source).astype(F32))
            places.append((q, t))
        rows = back_ref[:, group].reshape(devices * per, width)
        active = jnp.dot(
            jnp.concatenate(chosen, axis=0).astype(BF), rows, preferred_element_type=F32
        )
        for r, (q, t) in enumerate(places):
            out_ref[q, t] = (gates[r] * active[r * top : (r + 1) * top]).astype(BF)


def swap(x, axis, size, mask):
    return lax.ppermute(x, axis, [(i, i ^ mask) for i in range(size)])


def local_call(kernel, name, outs, *args, hbm=(), scratch=(), mib=24, flops=10**9):
    return pl.pallas_call(
        kernel,
        out_shape=outs,
        in_specs=[HBM if i in hbm else VMEM for i in range(len(args))],
        out_specs=jax.tree.map(lambda _: VMEM, outs),
        scratch_shapes=scratch,
        name=name,
        compiler_params=params(mib),
        cost_estimate=pl.CostEstimate(flops=flops, bytes_accessed=1, transcendentals=0),
    )(*args)


def fetched(*args, more=0):
    return tuple(pltpu.VMEM(x.shape, x.dtype) for x in args) + (
        pltpu.SemaphoreType.DMA((len(args) + more,)),
    )


def after(x, other):
    return lax.optimization_barrier((x, other))[0]


def per_device(queries, kv_pages, page_tables, lengths, owners, up_values, out_proj, residual,
               verify_states, norm_gain, route_ids, route_weights, expert_up):
    rows, _, key_width = queries.shape
    verify_rows, width = residual.shape
    n_expert, n_dp = lax.axis_size("expert"), lax.axis_size("dp")
    experts = n_expert * n_dp
    hidden = expert_up.shape[2]
    far = n_expert // NEAR
    far_groups = [[f * NEAR + n for f in range(far)] for n in range(NEAR)]
    shape = jax.ShapeDtypeStruct

    operands = (
        page_tables.T,
        lengths.reshape(1, rows),
        owners.reshape(1, rows),
        queries.reshape(rows, key_width),
        up_values[0],
        out_proj[0],
        kv_pages.reshape(-1, key_width),
    )
    partial_sums = local_call(
        functools.partial(attention_kernel, verify_rows),
        "attention",
        shape((far, NEAR * verify_rows, width), BF),
        *operands,
        hbm=range(7),
        scratch=fetched(*operands, more=KV_CHUNKS - 1),
        mib=60,
        flops=4000000000,
    )
    parts = lax.all_to_all(
        partial_sums, "expert", split_axis=0, concat_axis=0, tiled=True,
        axis_index_groups=far_groups,
    )
    near_sum = local_call(
        far_sum_kernel, "far_sum", shape((NEAR * verify_rows, width), BF), parts, residual, flops=1000000000,
    )
    tokens = local_call(
        norm_draft_kernel,
        "norm_draft",
        shape((far, NEAR * verify_rows, width), BF),
        near_sum,
        swap(near_sum, "expert", n_expert, 1),
        after(norm_gain, partial_sums).reshape(1, width),
    )
    draft = lax.all_to_all(
        tokens, "expert", split_axis=0, concat_axis=0, tiled=True, axis_index_groups=far_groups
    )

    masks = [n_expert // 2] + [1 << i for i in range(n_expert.bit_length() - 2)]
    gathered, codes = verify_states.reshape(-1, width), [0]
    other = swap(verify_states, "expert", n_expert, masks[0]).reshape(-1, width)
    for step, mask in enumerate(masks):
        if step:
            other = swap(gathered, "expert", n_expert, mask)
        if step < len(masks) - 2:
            gathered = gathered
        elif step < len(masks) - 1:
            gathered = after(gathered, near_sum)
        else:
            gathered = after(gathered, tokens)
        gathered = jnp.concatenate([gathered, other], axis=0)
        codes += [code ^ (mask * n_dp) for code in codes]
    gathered_other = swap(gathered, "dp", n_dp, 1)
    codes += [code ^ 1 for code in codes]
    token_rows = experts * verify_rows * VERIFY
    active = local_call(
        functools.partial(expert_kernel, codes),
        "expert",
        shape((experts, VERIFY, verify_rows, hidden), BF),
        draft, swap(draft, "dp", n_dp, 1), gathered, gathered_other,
        after(norm_gain, partial_sums).reshape(1, width), expert_up[0],
        hbm=(5,),
        scratch=(
            pltpu.VMEM((width, hidden), BF),
            pltpu.VMEM((token_rows, width), BF),
            pltpu.SemaphoreType.DMA((CHUNKS,)),
        ),
        mib=52,
        flops=4 * 10**9,
    )
    back = lax.all_to_all(active, ("expert", "dp"), split_axis=0, concat_axis=0, tiled=True)
    return local_call(
        select_kernel,
        "select",
        shape((verify_rows, VERIFY, route_ids.shape[2], hidden), BF),
        route_ids.transpose(1, 0, 2), route_weights.transpose(1, 0, 2), back,
    )


def solution(mesh):
    placed = (
        P(("groups", "dp"), "expert", None),
        P(("groups", "dp"), None, None),
        P(("groups", "dp"), None),
        P(("groups", "dp")),
        P(("groups", "dp")),
        P("expert", None, None),
        P("expert", None, None),
        P(("groups", "expert", "dp"), None),
        P(("groups", "expert", "dp"), None, None),
        P(),
        P(("groups", "expert", "dp"), None, None),
        P(("groups", "expert", "dp"), None, None),
        P(("expert", "dp"), None, None),
    )
    return jax.shard_map(
        per_device,
        mesh=mesh,
        in_specs=placed,
        out_specs=P(("groups", "expert", "dp"), None, None, None),
        check_vma=False,
    )
```

```python
import functools

import jax
import jax.numpy as jnp
from jax import lax
from jax.experimental import pallas as pl
from jax.experimental.pallas import tpu as pltpu
from jax.sharding import PartitionSpec as P

LATENT = 512
ROPE = 64
VHEAD = 128
VERIFY = 3
PAGES = 32
NEAR = 2
CHUNKS = 7
KV_CHUNKS = 1
ROW_BLOCK = 256
BF = jnp.bfloat16
F32 = jnp.float32
VMEM = pl.BlockSpec(memory_space=pltpu.VMEM)
HBM = pl.BlockSpec(memory_space=pltpu.HBM)


def params(mib=40):
    return pltpu.CompilerParams(vmem_limit_bytes=mib * 1024 * 1024)


def as_column(row, size):
    eye = lax.broadcasted_iota(jnp.int32, (size, size), 0) == lax.broadcasted_iota(
        jnp.int32, (size, size), 1
    )
    return jnp.sum(jnp.where(eye, row, 0), axis=1, keepdims=True)


def fetch(sources, targets, semaphores):
    copies = [
        pltpu.make_async_copy(source, target, semaphores.at[i])
        for i, (source, target) in enumerate(zip(sources, targets))
    ]
    for copy in copies:
        copy.start()
    return copies


def attention_kernel(per_owner, *refs):
    sources, sum_ref, targets, semaphores = refs[:7], refs[7], refs[8:15], refs[15]
    table_ref, length_ref, owner_ref, q_ref, up_ref, out_ref, kv_ref = targets
    small = fetch(sources[:4], targets[:4], semaphores)
    part = kv_ref.shape[0] // KV_CHUNKS
    chunks = [
        pltpu.make_async_copy(
            sources[6].at[pl.ds(i * part, part)], kv_ref.at[pl.ds(i * part, part)], semaphores.at[6 + i]
        )
        for i in range(KV_CHUNKS)
    ]
    for copy in chunks:
        copy.start()
    weights = fetch(sources[4:6], targets[4:6], semaphores.at[pl.ds(4, 2)])
    rows = q_ref.shape[0]
    tokens = kv_ref.shape[0]
    slots = table_ref.shape[0]
    page_len = tokens // PAGES
    token = lax.broadcasted_iota(jnp.int32, (1, tokens), 1)
    page, offset = token // page_len, token % page_len
    position = jnp.full((rows, tokens), 1 << 24, jnp.int32)
    for copy in small:
        copy.wait()
    for slot in range(slots):
        named = as_column(table_ref[slot : slot + 1, :], rows)
        position = jnp.where(named == page, slot * page_len + offset, position)
    visible = position < as_column(length_ref[...], rows)
    owner = owner_ref[...]
    first = lax.broadcasted_iota(jnp.int32, (rows, rows), 0)
    second = lax.broadcasted_iota(jnp.int32, (rows, rows), 1)
    before = (as_column(owner, rows) == owner) & (first < second)
    target = owner * per_owner + jnp.sum(before.astype(jnp.int32), axis=0, keepdims=True)
    scores = []
    for i, copy in enumerate(chunks):
        copy.wait()
        scores.append(
            lax.dot_general(
                q_ref[...],
                kv_ref[i * part : (i + 1) * part],
                (((1,), (1,)), ((), ())),
                preferred_element_type=F32,
            )
        )
    scores = jnp.concatenate(scores, axis=1) * (VHEAD + ROPE) ** (-0.5)
    masked = jnp.where(visible, scores, -1e30)
    row_max = jnp.max(masked, axis=1, keepdims=True)
    exponent = jnp.where(visible, jnp.exp(masked - row_max), 0.0)
    attention = (exponent / jnp.sum(exponent, axis=1, keepdims=True)).astype(BF)
    context = jnp.dot(attention, kv_ref[:, :LATENT], preferred_element_type=F32).astype(BF)
    for copy in weights:
        copy.wait()
    values = jnp.dot(context, up_ref[...], preferred_element_type=F32).astype(BF)
    picked = jnp.dot((first == target).astype(BF), values, preferred_element_type=F32).astype(BF)
    summed = jnp.dot(picked, out_ref[...], preferred_element_type=F32).astype(BF)
    groups, per_group, _ = sum_ref.shape
    for e in range(groups):
        sum_ref[e] = summed[e * per_group : (e + 1) * per_group]


def normed(states, gain):
    scale = lax.rsqrt(jnp.mean(states * states, axis=-1, keepdims=True) + 1e-06)
    return (states * scale * gain).astype(BF)


def far_sum_kernel(parts_ref, residual_ref, out_ref):
    total = parts_ref[0].astype(F32)
    for e in range(1, parts_ref.shape[0]):
        total = total + parts_ref[e].astype(F32)
    residual = residual_ref[...].astype(F32)
    rows = residual.shape[0]
    near = lax.rem(lax.axis_index("expert"), NEAR)
    twice = jnp.concatenate([residual] * NEAR, axis=0)
    place = lax.broadcasted_iota(jnp.int32, twice.shape, 0) // rows
    out_ref[...] = (total + jnp.where(place == near, twice, 0.0)).astype(BF)


def norm_draft_kernel(mine_ref, theirs_ref, gain_ref, out_ref):
    states = mine_ref[...].astype(F32) + theirs_ref[...].astype(F32)
    tokens = normed(states, gain_ref[...])
    for c in range(out_ref.shape[0]):
        out_ref[c] = tokens


def expert_kernel(codes, draft_ref, draft_other_ref, verify_ref, verify_other_ref, gain_ref, weight_hbm, out_ref,
                  weight_ref, tokens_ref, semaphores):
    chunks = semaphores.shape[0]
    depth = weight_ref.shape[0] // chunks
    copies = [
        pltpu.make_async_copy(
            weight_hbm.at[pl.ds(i * depth, depth)], weight_ref.at[pl.ds(i * depth, depth)], semaphores.at[i]
        )
        for i in range(chunks)
    ]
    for copy in copies:
        copy.start()
    n_dp = lax.axis_size("dp")
    dp = lax.axis_index("dp")
    me = lax.axis_index("expert") * n_dp + dp
    groups, per_group, width = draft_ref.shape
    per = out_ref.shape[2]
    rows = groups * per_group
    tokens_ref[:rows] = draft_ref[...].reshape(rows, width)
    tokens_ref[rows : 2 * rows] = draft_other_ref[...].reshape(rows, width)
    gain = gain_ref[...].astype(F32)
    half = verify_ref.shape[0]
    for part, states_ref in enumerate((verify_ref, verify_other_ref)):
        for start in range(0, half, ROW_BLOCK):
            stop = min(start + ROW_BLOCK, half)
            place = 2 * rows + part * half
            tokens_ref[place + start : place + stop] = normed(states_ref[start:stop].astype(F32), gain)
    total = tokens_ref.shape[0]
    for first in range(0, total, ROW_BLOCK):
        last = min(first + ROW_BLOCK, total)
        product = 0.0
        for i, copy in enumerate(copies):
            if first == 0:
                copy.wait()
            part = slice(i * depth, (i + 1) * depth)
            product = product + jnp.dot(
                tokens_ref[first:last, part], weight_ref[part], preferred_element_type=F32
            )
        active = (product * jax.nn.sigmoid(product)).astype(BF)
        for unit in range(first // per, last // per):
            if unit * per < 2 * rows:
                part, e = divmod(unit, rows // per)
                target, t = n_dp * e + (dp ^ part), 0
            else:
                block, t = divmod(unit - 2 * rows // per, VERIFY - 1)
                target, t = me ^ codes[block], t + 1
            out_ref[target, t] = active[unit * per - first : unit * per - first + per]


def select_kernel(ids_ref, gates_ref, back_ref, out_ref):
    devices, groups, per, width = back_ref.shape
    top = ids_ref.shape[2]
    eye = lax.broadcasted_iota(jnp.int32, (top, top), 0) == lax.broadcasted_iota(
        jnp.int32, (top, top), 1
    )
    source = lax.broadcasted_iota(jnp.int32, (top, devices * per), 1)
    for group in range(groups):
        places, chosen, gates = [], [], []
        for r in range(per):
            if group == 0:
                q, t = r, 0
            else:
                q, t = divmod((group - 1) * per + r, VERIFY - 1)
                t += 1
            ids = jnp.sum(jnp.where(eye, ids_ref[t, q : q + 1, :], 0), axis=1, keepdims=True)
            gates.append(
                jnp.sum(jnp.where(eye, gates_ref[t, q : q + 1, :], 0.0), axis=1, keepdims=True)
            )
            chosen.append((ids * per + r == source).astype(F32))
            places.append((q, t))
        rows = back_ref[:, group].reshape(devices * per, width)
        active = jnp.dot(
            jnp.concatenate(chosen, axis=0).astype(BF), rows, preferred_element_type=F32
        )
        for r, (q, t) in enumerate(places):
            out_ref[q, t] = (gates[r] * active[r * top : (r + 1) * top]).astype(BF)


def swap(x, axis, size, mask):
    return lax.ppermute(x, axis, [(i, i ^ mask) for i in range(size)])


def local_call(kernel, name, outs, *args, hbm=(), scratch=(), mib=24, flops=10**9):
    return pl.pallas_call(
        kernel,
        out_shape=outs,
        in_specs=[HBM if i in hbm else VMEM for i in range(len(args))],
        out_specs=jax.tree.map(lambda _: VMEM, outs),
        scratch_shapes=scratch,
        name=name,
        compiler_params=params(mib),
        cost_estimate=pl.CostEstimate(flops=flops, bytes_accessed=1, transcendentals=0),
    )(*args)


def fetched(*args, more=0):
    return tuple(pltpu.VMEM(x.shape, x.dtype) for x in args) + (
        pltpu.SemaphoreType.DMA((len(args) + more,)),
    )


def after(x, other):
    return lax.optimization_barrier((x, other))[0]


def per_device(queries, kv_pages, page_tables, lengths, owners, up_values, out_proj, residual,
               verify_states, norm_gain, route_ids, route_weights, expert_up):
    rows, _, key_width = queries.shape
    verify_rows, width = residual.shape
    n_expert, n_dp = lax.axis_size("expert"), lax.axis_size("dp")
    experts = n_expert * n_dp
    hidden = expert_up.shape[2]
    far = n_expert // NEAR
    far_groups = [[f * NEAR + n for f in range(far)] for n in range(NEAR)]
    shape = jax.ShapeDtypeStruct

    operands = (
        page_tables.T,
        lengths.reshape(1, rows),
        owners.reshape(1, rows),
        queries.reshape(rows, key_width),
        up_values[0],
        out_proj[0],
        kv_pages.reshape(-1, key_width),
    )
    partial_sums = local_call(
        functools.partial(attention_kernel, verify_rows),
        "attention",
        shape((far, NEAR * verify_rows, width), BF),
        *operands,
        hbm=range(7),
        scratch=fetched(*operands, more=KV_CHUNKS - 1),
        mib=60,
        flops=4000000000,
    )
    parts = lax.all_to_all(
        partial_sums, "expert", split_axis=0, concat_axis=0, tiled=True,
        axis_index_groups=far_groups,
    )
    near_sum = local_call(
        far_sum_kernel, "far_sum", shape((NEAR * verify_rows, width), BF), parts, residual, flops=1000000000,
    )
    tokens = local_call(
        norm_draft_kernel,
        "norm_draft",
        shape((far, NEAR * verify_rows, width), BF),
        near_sum,
        swap(near_sum, "expert", n_expert, 1),
        after(norm_gain, partial_sums).reshape(1, width),
    )
    draft = lax.all_to_all(
        tokens, "expert", split_axis=0, concat_axis=0, tiled=True, axis_index_groups=far_groups
    )

    masks = [n_expert // 2] + [1 << i for i in range(n_expert.bit_length() - 2)]
    gathered, codes = verify_states.reshape(-1, width), [0]
    other = swap(verify_states, "expert", n_expert, masks[0]).reshape(-1, width)
    for step, mask in enumerate(masks):
        if step:
            other = swap(gathered, "expert", n_expert, mask)
        if step < len(masks) - 2:
            gathered = gathered
        elif step < len(masks) - 1:
            gathered = after(gathered, near_sum)
        else:
            gathered = after(gathered, tokens)
        gathered = jnp.concatenate([gathered, other], axis=0)
        codes += [code ^ (mask * n_dp) for code in codes]
    gathered_other = swap(gathered, "dp", n_dp, 1)
    codes += [code ^ 1 for code in codes]
    token_rows = experts * verify_rows * VERIFY
    active = local_call(
        functools.partial(expert_kernel, codes),
        "expert",
        shape((experts, VERIFY, verify_rows, hidden), BF),
        draft, swap(draft, "dp", n_dp, 1), gathered, gathered_other,
        after(norm_gain, partial_sums).reshape(1, width), expert_up[0],
        hbm=(5,),
        scratch=(
            pltpu.VMEM((width, hidden), BF),
            pltpu.VMEM((token_rows, width), BF),
            pltpu.SemaphoreType.DMA((CHUNKS,)),
        ),
        mib=52,
        flops=4 * 10**9,
    )
    back = lax.all_to_all(active, ("expert", "dp"), split_axis=0, concat_axis=0, tiled=True)
    return local_call(
        select_kernel,
        "select",
        shape((verify_rows, VERIFY, route_ids.shape[2], hidden), BF),
        route_ids.transpose(1, 0, 2), route_weights.transpose(1, 0, 2), back,
    )


def solution(mesh):
    placed = (
        P(("groups", "dp"), "expert", None),
        P(("groups", "dp"), None, None),
        P(("groups", "dp"), None),
        P(("groups", "dp")),
        P(("groups", "dp")),
        P("expert", None, None),
        P("expert", None, None),
        P(("groups", "expert", "dp"), None),
        P(("groups", "expert", "dp"), None, None),
        P(),
        P(("groups", "expert", "dp"), None, None),
        P(("groups", "expert", "dp"), None, None),
        P(("expert", "dp"), None, None),
    )
    return jax.shard_map(
        per_device,
        mesh=mesh,
        in_specs=placed,
        out_specs=P(("groups", "expert", "dp"), None, None, None),
        check_vma=False,
    )
```
